256 devices in a mesh: dp: 4 (over y), seq: 2 (over core), expert: 32 (over x, z).
Axes of the slice: x: 4, y: 4, z: 8, core: 2. Of those that a mesh axis runs over, the one named last changes fastest.
Arguments:
- tokens: bfloat16 [4096, 3584], P('expert', 'dp'), may hold values from -6 to 6
- cotangent: bfloat16 [4096, 3584], P('expert', 'dp'), may hold values from -6 to 6
- expert_ids: int32 [4096, 8], P('expert'), may hold values from 0 to 63, all different within a row; in each aligned block of 128 rows (0 to 127, 128 to 255, ...) at most 24 rows name the same one
- gate_weights: float32 [4096, 8], P('expert'), may hold values from 0.08 to 0.8
- gate_proj: bfloat16 [64, 3584, 1024], P('expert', 'dp', 'seq'), may hold values from -0.09375 to 0.09375
- up_proj: bfloat16 [64, 3584, 1024], P('expert', 'dp', 'seq'), may hold values from -0.09375 to 0.09375
- down_proj: bfloat16 [64, 1024, 3584], P('expert', 'seq', 'dp'), may hold values from -0.1875 to 0.1875
Outputs:
- grad_tokens: bfloat16 [4096, 3584], P('expert', 'dp')
- grad_gate: bfloat16 [64, 3584, 1024], P('expert', 'dp', 'seq')
- grad_up: bfloat16 [64, 3584, 1024], P('expert', 'dp', 'seq')
- grad_down: bfloat16 [64, 1024, 3584], P('expert', 'seq', 'dp')
The draws below stay inside these ranges and needn't reach their ends.
Inputs may be any that keep to these rules, and one draw needn't show every extreme that they name: `expert_ids`: each row names 8 different experts. Among the 128 tokens of one index of expert no expert is named by more than 24 of them, and in every draw some expert is named by exactly 24 tokens of some index.
All inputs are finite; a program needn't handle non-finite values.
Results may differ from the reference program's by a relative error of at most 0.0064.
Values may be sent and summed in bfloat16 or wider, within the bound.
No kernel may reach another device: no remote copies, remote signals or barrier semaphores. Data moves between devices by JAX's collectives and lax.ppermute only.
A program may use at most 128 MiB of HBM per device.

```python
import math
import jax
import jax.numpy as jnp
import numpy as np
from jax import lax

D = 3584
F = 1024
TOP = 8
TOK_DEV = 128
EXPERTS = 64
CAP = 24
TOKENS = 4096
N_EXPERT = 32


def steps_of(own_key, extent, shards, least, largest):
    loudness, own = 1.0, jax.random.fold_in(own_key, 6)
    for dim, blocks in shards:
        draws = jnp.exp(jax.random.uniform(jax.random.fold_in(own, dim), (blocks,), jnp.float32, least / len(shards), largest / len(shards)))
        loudness = loudness * jnp.repeat(draws, extent[dim] // blocks).reshape([-1 if axis == dim else 1 for axis in range(len(extent))])
    return loudness


def deal_out(rng, own, number, rows, count, top, bound, lean):
    sequence = jax.random.permutation(rng, count)
    crowded, ordinary = load_shares(count, rows * top, bound, lean, True), load_shares(count, rows * top, bound, lean, False)
    places = jnp.arange(count)

    def named(sizes, turn):
        used = int((sizes > 0).sum())
        fixed = max(1, used // 4)
        passed = fixed + (places - fixed + turn * (used - fixed)) % max(1, count - fixed)
        return jnp.zeros((count,), jnp.int32).at[sequence[jnp.where(places < fixed, places, passed)]].set(jnp.asarray(sizes, jnp.int32))

    sizes = jnp.where(number % 4 == 0, named(crowded, number // 4), named(ordinary, number - number // 4 - 1))
    mixed = jax.random.permutation(jax.random.fold_in(own, 3), count)
    donor, taker = mixed[0:count // 2 * 2:2], mixed[1:count // 2 * 2:2]
    slack = jnp.minimum(sizes[donor] - 1, bound - sizes[taker]) // 2
    slack = jnp.where((donor == sequence[0]) | (taker == sequence[0]) | (sizes[taker] == 0), 0, jnp.maximum(slack, 0))
    passed = jax.random.randint(jax.random.fold_in(own, 4), (count // 2,), 0, 1 << 20) % (slack + 1)
    sizes = sizes.at[donor].add(-passed).at[taker].add(passed)
    items = jnp.searchsorted(jnp.cumsum(sizes), jnp.arange(rows * top), side="right").astype(jnp.int32)
    grid = items.reshape(top, rows).T
    grid = grid[jax.random.permutation(jax.random.fold_in(own, 1), rows)]
    turn = jax.random.randint(jax.random.fold_in(own, 2), (rows, 1), 0, top)
    return jnp.take_along_axis(grid, (jnp.arange(top)[None, :] + turn) % top, axis=1)


def load_shares(amount, total, bound, slope, full):
    weights = [(1 << 20) // math.isqrt(grade ** slope) + 1 for grade in range(1, amount + 1)]
    largest = bound if full else min(bound, max(-(-total // amount), total * weights[0] // sum(weights)))
    least = 1 if total - largest >= amount - 1 else 0
    holding, spare = [largest] + [least] * (amount - 1), total - largest - least * (amount - 1)
    while spare > 0:
        movable = [i for i in range(1, amount) if holding[i] < largest] or [i for i in range(1, amount) if holding[i] < bound]
        pool, left = sum([weights[i] for i in movable]), spare
        for i in movable:
            extra = min(bound - holding[i], max(1, left * weights[i] // pool), spare)
            holding[i] = holding[i] + extra
            spare = spare - extra
    return np.array(holding)


def scatter_about(key, extent, spread, most, split=(), kind=jnp.bfloat16):
    entries = spread * jax.random.normal(key, extent, jnp.float32)
    if split:
        entries = entries * steps_of(key, extent, split, -0.22, 0.18)
    return jnp.clip(entries, -most, most).astype(kind)


def setup_inputs(seed: int = 0) -> dict:
    keys = jax.random.split(jax.random.key(seed), 8)
    tokens = scatter_about(keys[0], (TOKENS, D), 1.0, 6.0, ((0, 32), (1, 4)))
    cotangent = scatter_about(keys[1], (TOKENS, D), 1.0, 6.0, ((0, 32), (1, 4)))
    expert_ids_keys = jax.random.split(jax.random.fold_in(keys[2], 1), TOKENS // TOK_DEV)
    expert_ids_turns = jax.random.permutation(jax.random.fold_in(keys[2], 3), TOKENS // TOK_DEV)
    expert_ids = jax.vmap(lambda own, number: deal_out(jax.random.fold_in(keys[2], 2), own, number, TOK_DEV, EXPERTS, TOP, CAP, 2))(expert_ids_keys, expert_ids_turns).reshape((TOKENS, TOP))
    gate_weights = jnp.clip(jnp.exp(math.log(0.8) - 2.3025851 * jax.random.uniform(keys[3], (TOKENS, TOP), jnp.float32) ** steps_of(keys[3], (TOKENS, TOP), ((0, 32),), -0.2, 0.2)), 0.08, 0.8)
    gate_proj = scatter_about(keys[4], (EXPERTS, D, F), D ** -0.5, 0.09375, ((0, 32), (1, 4), (2, 2)))
    up_proj = scatter_about(keys[5], (EXPERTS, D, F), D ** -0.5, 0.09375, ((0, 32), (1, 4), (2, 2)))
    down_proj = scatter_about(keys[6], (EXPERTS, F, D), F ** -0.5, 0.1875, ((0, 32), (1, 2), (2, 4)))
    return {"tokens": tokens, "cotangent": cotangent, "expert_ids": expert_ids, "gate_weights": gate_weights, "gate_proj": gate_proj, "up_proj": up_proj, "down_proj": down_proj}


def expert_terms(xrows, wrows, wg, wu, wd):
    g = jnp.dot(xrows, wg, preferred_element_type=jnp.float32)
    u = jnp.dot(xrows, wu, preferred_element_type=jnp.float32)
    sig = jax.nn.sigmoid(g)
    act = g * sig
    hidden = (act * u).astype(jnp.bfloat16)
    dh = lax.dot_general(wrows, wd, (((1,), (1,)), ((), ())), preferred_element_type=jnp.float32)
    grad_u = (dh * act).astype(jnp.bfloat16)
    grad_g = (dh * u * sig * (1.0 + g * (1.0 - sig))).astype(jnp.bfloat16)
    dwd = lax.dot_general(hidden, wrows, (((0,), (0,)), ((), ())), preferred_element_type=jnp.float32)
    dwg = lax.dot_general(xrows, grad_g, (((0,), (0,)), ((), ())), preferred_element_type=jnp.float32)
    dwu = lax.dot_general(xrows, grad_u, (((0,), (0,)), ((), ())), preferred_element_type=jnp.float32)
    back = lax.dot_general(grad_g, wg, (((1,), (1,)), ((), ())), preferred_element_type=jnp.float32)
    back = back + lax.dot_general(grad_u, wu, (((1,), (1,)), ((), ())), preferred_element_type=jnp.float32)
    return dwg, dwu, dwd, back


def reference(tokens, cotangent, expert_ids, gate_weights, gate_proj, up_proj, down_proj):
    total = TOKENS * TOP
    flat_ids = expert_ids.reshape(total)
    flat_gates = jnp.concatenate([gate_weights.reshape(total), jnp.zeros((1,), jnp.float32)])
    x_padded = jnp.concatenate([tokens, jnp.zeros((1, D), tokens.dtype)], axis=0)
    dy_padded = jnp.concatenate([cotangent, jnp.zeros((1, D), cotangent.dtype)], axis=0)
    most_rows = N_EXPERT * CAP

    def per_expert(accum, expert):
        index = jnp.nonzero(flat_ids == expert, size=most_rows, fill_value=total)[0].astype(jnp.int32)
        owner = jnp.where(index < total, index // TOP, TOKENS).astype(jnp.int32)
        xrows = x_padded[owner]
        wrows = (flat_gates[index][:, None] * dy_padded[owner].astype(jnp.float32)).astype(jnp.bfloat16)
        dwg, dwu, dwd, back = expert_terms(xrows, wrows, gate_proj[expert], up_proj[expert], down_proj[expert])
        rounded = lax.optimization_barrier(back.astype(jnp.bfloat16))
        accum = accum.at[owner].add(rounded.astype(jnp.float32))
        return accum, (dwg.astype(jnp.bfloat16), dwu.astype(jnp.bfloat16), dwd.astype(jnp.bfloat16))

    start = jnp.zeros((TOKENS + 1, D), jnp.float32)
    accum, grads = lax.scan(per_expert, start, jnp.arange(EXPERTS, dtype=jnp.int32))
    return accum[:TOKENS].astype(jnp.bfloat16), grads[0], grads[1], grads[2]
```

```python
import functools
import jax
import jax.numpy as jnp
from jax import lax
from jax.experimental import pallas as pl
from jax.experimental.pallas import tpu as pltpu
from jax.sharding import Mesh, PartitionSpec as P

BF = jnp.bfloat16
F32 = jnp.float32
NX, NZ, NY = 4, 8, 4
TB = 128
CAP = 24
QR = 48
MR = 192
DC = 896
FH = 512
META = 128
CHUNKS = ((0, 1), (3, 2))
VMEM = pl.BlockSpec(memory_space=pltpu.VMEM)
SMEM = pl.BlockSpec(memory_space=pltpu.SMEM)
NN = (((1,), (0,)), ((), ()))
NT = (((1,), (1,)), ((), ()))
TN = (((0,), (0,)), ((), ()))


def dot(a, b, dims=NN):
    return lax.dot_general(a, b, dims, preferred_element_type=F32)


def kernel_call(body, outs, n_in, scratch=(), flops=0, moved=0, name=None, smem=True):
    return pl.pallas_call(
        body,
        out_shape=[jax.ShapeDtypeStruct(s, t) for s, t in outs],
        in_specs=([SMEM] if smem else []) + [VMEM] * n_in,
        out_specs=[VMEM] * len(outs),
        scratch_shapes=[pltpu.VMEM(s, t) for s, t in scratch],
        compiler_params=pltpu.CompilerParams(vmem_limit_bytes=48 * 2**20),
        cost_estimate=pl.CostEstimate(flops=flops, bytes_accessed=moved, transcendentals=0),
        name=name,
    )


def first(y, s):
    return y ^ 1 if s == 0 else 3 - y


def second(y, s):
    return 3 - y if s == 0 else y ^ 1


def to_first(v):
    return lax.ppermute(
        v, ("dp", "seq"), [(y * 2 + s, first(y, s) * 2 + s) for y in range(NY) for s in range(2)]
    )


def to_second(v):
    return lax.ppermute(
        v, ("dp", "seq"), [(y * 2 + s, second(y, s) * 2 + s) for y in range(NY) for s in range(2)]
    )


def along_z(v, far):
    pairs = [(z, (z + far) % NZ) for z in range(NZ)]
    pairs += [(NZ + z, NZ + (z - far) % NZ) for z in range(NZ)]
    return lax.ppermute(v, ("seq", "ez"), pairs)


def along_x(v, far):
    return lax.ppermute(v, "ex", [(x, (x + far) % NX) for x in range(NX)])


def swap(v):
    return lax.ppermute(v, "seq", [(0, 1), (1, 0)])


def fill(dst, own, r1, r2, r3, r4, sw):
    dst[0:128] = own[:, :DC]
    dst[128:256] = r1[:, :DC]
    dst[256:384] = r2[:, :DC]
    dst[384:512] = r3[:, :DC]
    dst[512:576] = r4[:, :DC]
    dst[576:640] = sw[384:448, :DC]
    dst[640:1024] = sw[0:384, :DC]


def onehot(slots, d, b):
    row = slots[d * NZ + b : d * NZ + b + 1, :]
    return lax.broadcasted_iota(jnp.int32, (MR, TB), 0).astype(F32) == row


def pick_x(info, own, r1, r2, r3, r4, sw, m0, m1, m2, m3, slots, gates, rows, taken, hot):
    fill(rows, own, r1, r2, r3, r4, sw)
    for b in range(NZ):
        if b == 0:
            meta = own[:, DC:]
        elif b < 4:
            meta = (r1, r2, r3)[b - 1][:, DC:]
        elif b == 4:
            meta = jnp.concatenate([r4[:, DC:], sw[384:448, DC:]], axis=0)
        else:
            meta = sw[(b - 5) * TB : (b - 4) * TB, DC:]
        turned = jnp.transpose(meta.astype(F32))
        ids = turned[0:8]
        gate = turned[8:16] + turned[16:24] + turned[24:32]
        for d in range(NX):
            named = ids == info[d].astype(F32)
            at = slice(d * NZ + b, d * NZ + b + 1)
            taken[at, :] = jnp.sum(named.astype(F32), axis=0, keepdims=True)
            gates[at, :] = jnp.sum(jnp.where(named, gate, 0.0), axis=0, keepdims=True)
    upper = lax.broadcasted_iota(jnp.int32, (TB, TB), 0) < lax.broadcasted_iota(
        jnp.int32, (TB, TB), 1
    )
    rank = dot(taken[...].astype(BF), upper.astype(F32).astype(BF))
    for d in range(NX):
        for b in range(NZ):
            at = d * NZ + b
            base = (info[4 + b // 2] + (b % 2) * CAP).astype(F32)
            slots[at : at + 1, :] = jnp.where(
                taken[at : at + 1, :] > 0.5, rank[at : at + 1, :] + base, -1.0
            )
    for d, out in enumerate((m0, m1, m2, m3)):
        for b in range(NZ):
            hot[:, b * TB : (b + 1) * TB] = onehot(slots, d, b).astype(F32).astype(BF)
        out[...] = dot(hot[...], rows[...]).astype(BF)


def pick_w(slots, gates, own, r1, r2, r3, r4, sw, m0, m1, m2, m3, rows, hot):
    fill(rows, own, r1, r2, r3, r4, sw)
    for d, out in enumerate((m0, m1, m2, m3)):
        total = jnp.zeros((MR, TB), F32)
        for b in range(NZ):
            mask = onehot(slots, d, b)
            at = d * NZ + b
            total = total + jnp.where(mask, gates[at : at + 1, :], 0.0)
            hot[:, b * TB : (b + 1) * TB] = mask.astype(F32).astype(BF)
        gate = jnp.sum(total, axis=1, keepdims=True)
        out[...] = (gate * dot(hot[...], rows[...])).astype(BF)


def combine(slots, b0, b1, b2, b3, own, mine, theirs, rows, hot):
    for d, ref in enumerate((b0, b1, b2, b3)):
        rows[d * MR : (d + 1) * MR] = ref[...]
        for b in range(NZ):
            hot[d * MR : (d + 1) * MR, b * TB : (b + 1) * TB] = (
                onehot(slots, d, b).astype(F32).astype(BF)
            )
    for b in range(NZ):
        part = dot(hot[:, b * TB : (b + 1) * TB], rows[...], TN)
        if b == 0:
            own[...] = part
        elif b < 4:
            mine[(b - 1) * TB : b * TB] = part
        elif b == 4:
            mine[384:448] = part[:64]
            theirs[384:448] = part[64:].astype(BF)
        else:
            theirs[(b - 5) * TB : (b - 4) * TB] = part.astype(BF)


def join(mine, got, o1, o2, o3, o4):
    for i, out in enumerate((o1, o2, o3)):
        at = slice(i * TB, (i + 1) * TB)
        out[...] = (mine[at] + got[at].astype(F32)).astype(BF)
    o4[...] = (mine[384:448] + got[384:448].astype(F32)).astype(BF)


def by_quarter(dst, refs, start=0):
    n = len(refs)
    for q in range(4):
        for i, ref in enumerate(refs):
            dst[start + (q * n + i) * QR : start + (q * n + i + 1) * QR] = ref[
                q * QR : (q + 1) * QR
            ]


def up_products(n, info, *refs):
    xs, (wg, wgo, wu, wuo, keep, send, rows) = refs[:n], refs[n:]
    s = info[8]
    by_quarter(rows, xs)
    half = n * 2 * QR
    for k, (own, other) in enumerate(((wg, wgo), (wu, wuo))):
        a = dot(rows[...], own[s])
        keep[k, :, :FH] = a[:half]
        send[k, :, :FH] = a[half:].astype(BF)
        a = dot(rows[...], other[...])
        keep[k, :, FH:] = a[:half]
        send[k, :, FH:] = a[half:].astype(BF)


def down_products(n, info, *refs):
    ws, (wd, wdo, keep, send, rows) = refs[:n], refs[n:]
    s = info[8]
    by_quarter(rows, ws)
    half = n * 2 * QR
    a = dot(rows[...], wd[s], NT)
    keep[:, :FH] = a[:half]
    send[:, :FH] = a[half:].astype(BF)
    a = dot(rows[...], wdo[...], NT)
    keep[:, FH:] = a[:half]
    send[:, FH:] = a[half:].astype(BF)


def halve(keep, got, mine, send):
    m = keep.shape[-2] // 2
    mine[...] = keep[..., :m, :] + got[..., :m, :].astype(F32)
    send[...] = (keep[..., m:, :] + got[..., m:, :].astype(F32)).astype(BF)


def terms(gu, gu2, dh, dh2, out):
    g = gu[0] + gu2[0].astype(F32)
    u = gu[1] + gu2[1].astype(F32)
    h = dh[...] + dh2[...].astype(F32)
    s = jax.nn.sigmoid(g)
    act = g * s
    out[0] = (act * u).astype(BF)
    out[1] = (h * u * s * (1.0 + g * (1.0 - s))).astype(BF)
    out[2] = (h * act).astype(BF)


def back_rows(n, info, a0, a1, a2, a3, wg, wgo, wu, wuo, *refs):
    outs, (dg, du) = refs[:n], refs[n:]
    s = info[8]
    m = n * QR
    for q, a in enumerate((a0, a1, a2, a3)):
        dg[q * m : (q + 1) * m] = a[1]
        du[q * m : (q + 1) * m] = a[2]
    total = dot(dg[:, :FH], wg[s], NT) + dot(dg[:, FH:], wgo[...], NT)
    total = total + dot(du[:, :FH], wu[s], NT) + dot(du[:, FH:], wuo[...], NT)
    total = total.astype(BF)
    for q in range(4):
        for i, out in enumerate(outs):
            out[q * QR : (q + 1) * QR] = total[(q * n + i) * QR : (q * n + i + 1) * QR]


def weight_grad(which, info, *refs):
    xs, parts = refs[:4], refs[4 : 4 + 4 * len(CHUNKS)]
    out, send, rows, cols = refs[4 + 4 * len(CHUNKS) :]
    s = info[8]
    start = 0
    for c, chunk in enumerate(CHUNKS):
        n = len(chunk)
        by_quarter(rows, [xs[d] for d in chunk], start)
        for q in range(4):
            at = start + q * n * QR
            cols[at : at + n * QR] = parts[4 * c + q][which]
        start += n * MR
    if which == 0:
        out[s] = dot(cols[:, :FH], rows[...], TN).astype(BF)
        send[...] = dot(cols[:, FH:], rows[...], TN).astype(BF)
    else:
        out[s] = dot(rows[...], cols[:, :FH], TN).astype(BF)
        send[...] = dot(rows[...], cols[:, FH:], TN).astype(BF)


def on_device(tokens, cotangent, expert_ids, gate_weights, gate_proj, up_proj, down_proj):
    y, s = lax.axis_index("dp"), lax.axis_index("seq")
    x, z = lax.axis_index("ex"), lax.axis_index("ez")
    p1 = jnp.where(s == 0, y ^ 1, 3 - y)
    p2 = jnp.where(s == 0, 3 - y, y ^ 1)
    experts = [2 * (((x + d) % NX) * NZ + z) + s for d in range(NX)]
    bases = [
        QR * jnp.where(q == y, 0, jnp.where(q == p2, 1, jnp.where(q == p1, 2, 3)))
        for q in range(4)
    ]
    info = jnp.stack([jnp.asarray(v, jnp.int32) for v in [*experts, *bases, s]])

    high = lax.reduce_precision(gate_weights, 8, 7)
    rest = gate_weights - high
    middle = lax.reduce_precision(rest, 8, 7)
    low = rest - middle
    meta = jnp.concatenate([expert_ids.astype(F32), high, middle, low], axis=1).astype(BF)
    packed = jnp.concatenate([tokens, jnp.pad(meta, ((0, 0), (0, META - 32)))], axis=1)

    def gather(block):
        near = [along_z(block, far) for far in (1, 2, 3)]
        part = lax.dynamic_slice_in_dim(block, s * (TB // 2), TB // 2, 0)
        near.append(along_z(part, 4))
        return [block, *near, swap(jnp.concatenate(near, axis=0))]

    blocks_x = gather(packed)
    blocks_w = gather(cotangent)

    def others(w):
        return swap(lax.dynamic_index_in_dim(w, 1 - s, 0, keepdims=False))

    gate_o, up_o, down_o = others(gate_proj), others(up_proj), others(down_proj)

    message = ((MR, DC), BF)
    *to_x, slots, gates = kernel_call(
        pick_x,
        [message] * 4 + [((32, TB), F32)] * 2,
        6,
        [((1024, DC), BF), ((32, TB), F32), ((MR, 1024), BF)],
        flops=2 * 768 * 1024 * 896,
        moved=4_000_000,
        name="pick_x",
    )(info, *blocks_x)
    to_w = kernel_call(
        pick_w,
        [message] * 4,
        8,
        [((1024, DC), BF), ((MR, 1024), BF)],
        flops=2 * 768 * 1024 * 896,
        moved=4_000_000,
        name="pick_w",
        smem=False,
    )(slots, gates, *blocks_w)
    xs = [m if d == 0 else along_x(m, d) for d, m in enumerate(to_x)]
    ws = [m if d == 0 else along_x(m, d) for d, m in enumerate(to_w)]

    parts, returned = [], [None] * NX
    for chunk in CHUNKS:
        n = len(chunk)
        half = n * 2 * QR
        keep, send = kernel_call(
            functools.partial(up_products, n),
            [((2, half, 1024), F32), ((2, half, 1024), BF)],
            n + 4,
            [((n * MR, DC), BF)],
            flops=4 * n * MR * DC * 1024,
            moved=4_000_000 + n * 1_500_000,
            name="up_products",
        )(info, *[xs[d] for d in chunk], gate_proj, gate_o, up_proj, up_o)
        gu, send = kernel_call(
            halve,
            [((2, half // 2, 1024), F32), ((2, half // 2, 1024), BF)],
            2,
            moved=n * 2_000_000,
            name="halve_gu",
            smem=False,
        )(keep, to_first(send))
        gu2 = to_second(send)
        keep, send = kernel_call(
            functools.partial(down_products, n),
            [((half, 1024), F32), ((half, 1024), BF)],
            n + 2,
            [((n * MR, DC), BF)],
            flops=2 * n * MR * DC * 1024,
            moved=2_000_000 + n * 1_000_000,
            name="down_products",
        )(info, *[ws[d] for d in chunk], down_proj, down_o)
        dh, send = kernel_call(
            halve,
            [((half // 2, 1024), F32), ((half // 2, 1024), BF)],
            2,
            moved=n * 1_000_000,
            name="halve_dh",
            smem=False,
        )(keep, to_first(send))
        dh2 = to_second(send)
        [own] = kernel_call(
            terms,
            [((3, half // 2, 1024), BF)],
            4,
            moved=n * 1_200_000,
            name="terms",
            smem=False,
        )(gu, gu2, dh, dh2)
        a1 = to_second(own)
        a2 = to_first(own)
        a3 = to_first(a1)
        parts.append([own, a1, a2, a3])
    for chunk, part in zip(CHUNKS, parts):
        n = len(chunk)
        rows = kernel_call(
            functools.partial(back_rows, n),
            [message] * n,
            8,
            [((n * MR, 1024), BF)] * 2,
            flops=4 * n * MR * DC * 1024,
            moved=4_000_000 + n * 1_500_000,
            name="back_rows",
        )(info, *part, gate_proj, gate_o, up_proj, up_o)
        for d, r in zip(chunk, rows):
            returned[d] = r if d == 0 else along_x(r, NX - d)

    flat = [a for part in parts for a in part]

    def weights(which, rows_of, shape):
        out, send = kernel_call(
            functools.partial(weight_grad, which),
            [((2, *shape), BF), (shape, BF)],
            4 + len(flat),
            [((4 * MR, DC), BF), ((4 * MR, 1024), BF)],
            flops=2 * 4 * MR * DC * 1024,
            moved=9_000_000,
            name="weight_grad",
        )(info, *rows_of, *flat)
        return lax.dynamic_update_slice(out, swap(send)[None], (1 - s, 0, 0))

    grad_down = weights(0, ws, (FH, DC))
    grad_gate = weights(1, xs, (DC, FH))
    grad_up = weights(2, xs, (DC, FH))

    own, mine, theirs = kernel_call(
        combine,
        [((TB, DC), F32), ((448, DC), F32), ((448, DC), BF)],
        5,
        [((4 * MR, DC), BF), ((4 * MR, 1024), BF)],
        flops=2 * 768 * 1024 * 896,
        moved=5_000_000,
        name="combine",
        smem=False,
    )(slots, *returned)
    homeward = kernel_call(
        join,
        [((TB, DC), BF)] * 3 + [((TB // 2, DC), BF)],
        2,
        moved=3_000_000,
        name="join",
        smem=False,
    )(mine, swap(theirs))
    homed = [along_z(v, -far) for v, far in zip(homeward, (1, 2, 3, 4))]
    total = own
    for v in homed[:3]:
        total = total + v.astype(F32)
    row = lax.broadcasted_iota(jnp.int32, (TB, 1), 0) // (TB // 2)
    last = homed[3].astype(F32)
    total = total + jnp.where(row == s, jnp.concatenate([last, last], axis=0), 0.0)
    grad_tokens = (total + swap(total)).astype(BF)
    return grad_tokens, grad_gate, grad_up, grad_down


def solution(mesh):
    parts = Mesh(mesh.devices.reshape(NY, 2, NX, NZ), ("dp", "seq", "ex", "ez"))
    expert = ("ex", "ez")
    in_specs = (
        P(expert, "dp"),
        P(expert, "dp"),
        P(expert, None),
        P(expert, None),
        P(expert, "dp", "seq"),
        P(expert, "dp", "seq"),
        P(expert, "seq", "dp"),
    )
    out_specs = (
        P(expert, "dp"),
        P(expert, "dp", "seq"),
        P(expert, "dp", "seq"),
        P(expert, "seq", "dp"),
    )
    return jax.shard_map(
        on_device, mesh=parts, in_specs=in_specs, out_specs=out_specs, check_vma=False
    )
```

```python
import functools
import jax
import jax.numpy as jnp
from jax import lax
from jax.experimental import pallas as pl
from jax.experimental.pallas import tpu as pltpu
from jax.sharding import Mesh, PartitionSpec as P

BF = jnp.bfloat16
F32 = jnp.float32
NX, NZ, NY = 4, 8, 4
TB = 128
CAP = 24
QR = 48
MR = 192
DC = 896
FH = 512
META = 128
CHUNKS = ((0,), (1, 3), (2,))
VMEM = pl.BlockSpec(memory_space=pltpu.VMEM)
SMEM = pl.BlockSpec(memory_space=pltpu.SMEM)
NN = (((1,), (0,)), ((), ()))
NT = (((1,), (1,)), ((), ()))
TN = (((0,), (0,)), ((), ()))


def dot(a, b, dims=NN):
    return lax.dot_general(a, b, dims, preferred_element_type=F32)


ANY = pl.BlockSpec(memory_space=pl.ANY)


class Queue:
    def __init__(self):
        self.last = None

    def __call__(
        self, body, outs, ins, scratch=(), name=None, after=(), hand=(), hbm=False, limit=48
    ):
        waits = list(after) + ([] if self.last is None else [self.last])
        n, k, h, m = len(ins), len(waits), len(hand), len(outs)

        def run(*refs):
            body(*refs[:n], *refs[n + k + h : n + k + h + m], *refs[n + k + 2 * h + m :])

        done = pl.pallas_call(
            run,
            out_shape=[jax.ShapeDtypeStruct(s, t) for s, t in outs]
            + [jax.ShapeDtypeStruct(v.shape, v.dtype) for v in hand],
            in_specs=[SMEM if v.shape == (9,) else ANY if hbm else VMEM for v in ins]
            + [ANY] * (k + h),
            out_specs=[VMEM] * m + [ANY] * h,
            scratch_shapes=[pltpu.VMEM(*v) if isinstance(v, tuple) else v for v in scratch],
            input_output_aliases={n + k + i: m + i for i in range(h)},
            compiler_params=pltpu.CompilerParams(vmem_limit_bytes=limit * 2**20),
            cost_estimate=pl.CostEstimate(flops=1, bytes_accessed=1, transcendentals=0),
            name=name,
        )(*ins, *waits, *hand)
        self.last = done[0]
        return done


def first(y, s):
    return y ^ 1 if s == 0 else 3 - y


def second(y, s):
    return 3 - y if s == 0 else y ^ 1


def to_first(v):
    return lax.ppermute(
        v, ("dp", "seq"), [(y * 2 + s, first(y, s) * 2 + s) for y in range(NY) for s in range(2)]
    )


def to_second(v):
    return lax.ppermute(
        v, ("dp", "seq"), [(y * 2 + s, second(y, s) * 2 + s) for y in range(NY) for s in range(2)]
    )


def along_z(v, far):
    pairs = [(z, (z + far) % NZ) for z in range(NZ)]
    pairs += [(NZ + z, NZ + (z - far) % NZ) for z in range(NZ)]
    return lax.ppermute(v, ("seq", "ez"), pairs)


def opposite(v):
    pairs = [(z, (z + 2) % NZ) for z in range(0, NZ, 2)]
    pairs += [(NZ + z, NZ + (z - 2) % NZ) for z in range(1, NZ, 2)]
    return lax.ppermute(v, ("seq", "ez"), pairs)


def swap_opposite(v):
    pairs = [(z, NZ + z) if z % 2 == 0 else (NZ + z, z) for z in range(NZ)]
    return lax.ppermute(v, ("seq", "ez"), pairs)


def along_x(v, far):
    return lax.ppermute(v, "ex", [(x, (x + far) % NX) for x in range(NX)])


def swap(v):
    return lax.ppermute(v, "seq", [(0, 1), (1, 0)])


def copy_all(pairs, sems):
    copies = [pltpu.make_async_copy(a, b, sems.at[i]) for i, (a, b) in enumerate(pairs)]
    for copy in copies:
        copy.start()
    for copy in copies:
        copy.wait()


def pack(info, tokens, cot, ids, gates, gate, up, down, out, weights, numbers, scale, meta, sems):
    t = 1 - info[8]
    copies = [
        pltpu.make_async_copy(a, b, sems.at[i])
        for i, (a, b) in enumerate(
            (
                (ids, numbers),
                (gates, scale),
                (tokens, out.at[:, :DC]),
                (cot, out.at[:, DC : 2 * DC]),
                (gate.at[t], weights.at[:DC]),
                (up.at[t], weights.at[DC : 2 * DC]),
                (down.at[t, :, :FH], weights.at[2 * DC : 2 * DC + FH]),
                (down.at[t, :, FH:], weights.at[2 * DC + FH :, : DC - FH]),
            )
        )
    ]
    for copy in copies:
        copy.start()
    meta[...] = jnp.zeros_like(meta)
    weights[2 * DC + FH :, DC - FH :] = jnp.zeros((FH, 2 * FH - DC), BF)
    copies[0].wait()
    copies[1].wait()
    high = scale[...].astype(BF).astype(F32)
    middle = (scale[...] - high).astype(BF).astype(F32)
    meta[0:8] = numbers[...].astype(F32)
    meta[8:16] = high
    meta[16:24] = middle
    meta[24:32] = (scale[...] - high) - middle
    out[:, 2 * DC :] = jnp.transpose(meta[...]).astype(BF)
    for copy in copies[2:]:
        copy.wait()


def place_grads(info, got, gate, up, down, token, gate_out, up_out, down_out, sems):
    t = 1 - info[8]
    copy_all(
        (
            (got.at[:DC], gate_out.at[t]),
            (got.at[DC : 2 * DC], up_out.at[t]),
            (got.at[2 * DC : 2 * DC + FH], down_out.at[t, :, :FH]),
            (got.at[2 * DC + FH :, : DC - FH], down_out.at[t, :, FH:]),
        ),
        sems,
    )


def bring_home(info, home, h1, h2, h3, h4, out):
    out[...] = home[...] + h1[...].astype(F32) + h2[...].astype(F32) + h3[...].astype(F32)
    at = pl.ds(pl.multiple_of(info[8] * (TB // 2), TB // 2), TB // 2)
    out[at] = out[at] + h4[...].astype(F32)


def finish(mine, other, out):
    out[...] = (mine[...] + other[...]).astype(BF)


def put_down(out, down):
    out[2 * DC : 2 * DC + FH] = down[:, :FH]
    out[2 * DC + FH :, : DC - FH] = down[:, FH:]
    out[2 * DC + FH :, DC - FH :] = jnp.zeros((FH, 2 * FH - DC), BF)


def onehot(slots, d, b):
    row = slots[d * NZ + b : d * NZ + b + 1, :]
    return lax.broadcasted_iota(jnp.int32, (MR, TB), 0).astype(F32) == row


def pick(info, own, r1, r2, r3, r4, s4, s1, s2, s3, m0, m1, m2, m3, slots, rows, taken, gates, hot):
    for b, block in enumerate((own, r1, r2, r3, r4, s1, s2, s3)):
        at = slice(b * TB, (b + 1) * TB)
        if b == 4:
            rows[at] = r4[:, : 2 * DC] + s4[:, : 2 * DC]
            meta = r4[:, 2 * DC :] + s4[:, 2 * DC :]
        else:
            rows[at] = block[:, : 2 * DC]
            meta = block[:, 2 * DC :]
        turned = jnp.transpose(meta.astype(F32))
        ids = turned[0:8]
        gate = turned[8:16] + turned[16:24] + turned[24:32]
        for d in range(NX):
            named = ids == info[d].astype(F32)
            at = slice(d * NZ + b, d * NZ + b + 1)
            taken[at, :] = jnp.sum(named.astype(F32), axis=0, keepdims=True)
            gates[at, :] = jnp.sum(jnp.where(named, gate, 0.0), axis=0, keepdims=True)
    upper = lax.broadcasted_iota(jnp.int32, (TB, TB), 0) < lax.broadcasted_iota(
        jnp.int32, (TB, TB), 1
    )
    rank = dot(taken[...].astype(BF), upper.astype(F32).astype(BF))
    for d in range(NX):
        for b in range(NZ):
            at = d * NZ + b
            base = (info[4 + b // 2] + (b % 2) * CAP).astype(F32)
            slots[at : at + 1, :] = jnp.where(
                taken[at : at + 1, :] > 0.5, rank[at : at + 1, :] + base, -1.0
            )
    for d, out in enumerate((m0, m1, m2, m3)):
        total = jnp.zeros((MR, TB), F32)
        for b in range(NZ):
            mask = onehot(slots, d, b)
            at = d * NZ + b
            total = total + jnp.where(mask, gates[at : at + 1, :], 0.0)
            hot[:, b * TB : (b + 1) * TB] = mask.astype(F32).astype(BF)
        gate = jnp.sum(total, axis=1, keepdims=True)
        out[:, :DC] = dot(hot[...], rows[:, :DC]).astype(BF)
        out[:, DC:] = (gate * dot(hot[...], rows[:, DC:])).astype(BF)


def combine(info, slots, b0, b1, b2, b3, own, mine, theirs, rows, hot, far):
    for d, ref in enumerate((b0, b1, b2, b3)):
        rows[d * MR : (d + 1) * MR] = ref[...]
        for b in range(NZ):
            hot[d * MR : (d + 1) * MR, b * TB : (b + 1) * TB] = (
                onehot(slots, d, b).astype(F32).astype(BF)
            )
    half = TB // 2
    for b in range(NZ):
        part = dot(hot[:, b * TB : (b + 1) * TB], rows[...], TN)
        if b == 0:
            own[...] = part
        elif b < 4:
            mine[(b - 1) * TB : b * TB] = part
        elif b == 4:
            far[...] = part
            mine[3 * TB :] = far[pl.ds(pl.multiple_of(info[8] * half, half), half)]
            theirs[3 * TB :] = far[pl.ds(pl.multiple_of((1 - info[8]) * half, half), half)].astype(BF)
        else:
            theirs[(b - 5) * TB : (b - 4) * TB] = part.astype(BF)


def join(mine, got, o1, o2, o3, o4):
    for i, out in enumerate((o1, o2, o3)):
        at = slice(i * TB, (i + 1) * TB)
        out[...] = (mine[at] + got[at].astype(F32)).astype(BF)
    o4[...] = (mine[384:448] + got[384:448].astype(F32)).astype(BF)


def by_quarter(dst, refs, start=0):
    n = len(refs)
    for q in range(4):
        for i, ref in enumerate(refs):
            dst[start + (q * n + i) * QR : start + (q * n + i + 1) * QR] = ref[
                q * QR : (q + 1) * QR
            ]


def products(n, info, *refs):
    messages, (wg, wu, wd, wo, keep, send, rows) = refs[:n], refs[n:]
    s = info[8]
    by_quarter(rows, messages)
    x, w = rows[:, :DC], rows[:, DC:]
    half = n * 2 * QR
    down = 2 * DC
    for k, a, b in (
        (0, lambda: dot(x, wg[s]), lambda: dot(x, wo[:DC])),
        (1, lambda: dot(x, wu[s]), lambda: dot(x, wo[DC:down])),
        (
            2,
            lambda: dot(w, wd[s], NT),
            lambda: dot(w[:, :FH], wo[down : down + FH], NT)
            + dot(w[:, FH:], wo[down + FH :, : DC - FH], NT),
        ),
    ):
        for at, f in ((0, a), (FH, b)):
            v = f()
            keep[k, :, at : at + FH] = v[:half]
            send[k, :, at : at + FH] = v[half:].astype(BF)


def halve(keep, got, mine, send):
    m = keep.shape[-2] // 2
    mine[...] = keep[..., :m, :] + got[..., :m, :].astype(F32)
    send[...] = (keep[..., m:, :] + got[..., m:, :].astype(F32)).astype(BF)


def terms(keep, got, out):
    g = keep[0] + got[0].astype(F32)
    u = keep[1] + got[1].astype(F32)
    h = keep[2] + got[2].astype(F32)
    s = jax.nn.sigmoid(g)
    act = g * s
    out[0] = (act * u).astype(BF)
    out[1] = (h * u * s * (1.0 + g * (1.0 - s))).astype(BF)
    out[2] = (h * act).astype(BF)


def back_rows(n, info, a0, a1, a2, a3, wg, wu, wo, *refs):
    outs, (dg, du) = refs[:n], refs[n:]
    s = info[8]
    m = n * QR
    for q, a in enumerate((a0, a1, a2, a3)):
        dg[q * m : (q + 1) * m] = a[1]
        du[q * m : (q + 1) * m] = a[2]
    total = dot(dg[:, :FH], wg[s], NT) + dot(dg[:, FH:], wo[:DC], NT)
    total = total + dot(du[:, :FH], wu[s], NT) + dot(du[:, FH:], wo[DC : 2 * DC], NT)
    total = total.astype(BF)
    for q in range(4):
        for i, out in enumerate(outs):
            out[q * QR : (q + 1) * QR] = total[(q * n + i) * QR : (q * n + i + 1) * QR]


def weight_grads(info, *refs):
    messages, parts = refs[:4], refs[4 : 4 + 4 * len(CHUNKS)]
    gate, up, down, send, rows, cols = refs[4 + 4 * len(CHUNKS) :]
    s = info[8]
    start = 0
    for c, chunk in enumerate(CHUNKS):
        n = len(chunk)
        by_quarter(rows, [messages[d] for d in chunk], start)
        for q in range(4):
            at = start + q * n * QR
            cols[:, at : at + n * QR] = parts[4 * c + q][...]
        start += n * MR
    x, w = rows[:, :DC], rows[:, DC:]
    down[s] = dot(cols[0, :, :FH], w, TN).astype(BF)
    put_down(send, dot(cols[0, :, FH:], w, TN).astype(BF))
    gate[s] = dot(x, cols[1, :, :FH], TN).astype(BF)
    send[:DC] = dot(x, cols[1, :, FH:], TN).astype(BF)
    up[s] = dot(x, cols[2, :, :FH], TN).astype(BF)
    send[DC : 2 * DC] = dot(x, cols[2, :, FH:], TN).astype(BF)


def on_device(tokens, cotangent, expert_ids, gate_weights, gate_proj, up_proj, down_proj):
    y, s = lax.axis_index("dp"), lax.axis_index("seq")
    x, z = lax.axis_index("ex"), lax.axis_index("ez")
    p1 = jnp.where(s == 0, y ^ 1, 3 - y)
    p2 = jnp.where(s == 0, 3 - y, y ^ 1)
    experts = [2 * (((x + d) % NX) * NZ + z) + s for d in range(NX)]
    bases = [
        QR * jnp.where(q == y, 0, jnp.where(q == p2, 1, jnp.where(q == p1, 2, 3)))
        for q in range(4)
    ]
    info = jnp.stack([jnp.asarray(v, jnp.int32) for v in [*experts, *bases, s]])

    queue = Queue()
    block = ((TB, DC), BF)

    weights = ((2 * DC + 2 * FH, FH), BF)
    message = ((MR, 2 * DC), BF)
    width = 2 * DC + META

    packed, others = queue(
        pack,
        [((TB, width), BF), weights],
        (
            info,
            tokens,
            cotangent,
            expert_ids.T,
            gate_weights.T,
            gate_proj,
            up_proj,
            down_proj,
        ),
        [
            ((8, TB), jnp.int32),
            ((8, TB), F32),
            ((META, TB), F32),
            pltpu.SemaphoreType.DMA((8,)),
        ],
        name="pack",
        hbm=True,
        limit=60,
    )
    r1, r2 = along_z(packed, 1), along_z(packed, 2)
    r3, r4 = along_z(r2, 1), opposite(r2)
    others = swap(others)
    *messages, slots = queue(
        pick,
        [message] * 4 + [((32, TB), F32)],
        (info, packed, r1, r2, r3, r4, swap_opposite(r4), swap(r1), swap(r2), swap(r3)),
        [((1024, 2 * DC), BF), ((32, TB), F32), ((32, TB), F32), ((MR, 1024), BF)],
        name="pick",
    )
    messages = [m if d == 0 else along_x(m, d) for d, m in enumerate(messages)]

    count = len(CHUNKS)
    sums, parts, returned = [None] * count, [None] * count, [None] * NX

    def multiply(c, *after):
        chunk = CHUNKS[c]
        n = len(chunk)
        keep, send = queue(
            functools.partial(products, n),
            [((3, n * 2 * QR, 1024), F32), ((3, n * 2 * QR, 1024), BF)],
            (info, *[messages[d] for d in chunk], gate_proj, up_proj, down_proj, others),
            [((n * MR, 2 * DC), BF)],
            after=after,
            name="products",
        )
        sums[c] = keep, to_first(send)

    def reduce(c, *after):
        m = len(CHUNKS[c]) * QR
        keep, send = queue(
            halve, [((3, m, 1024), F32), ((3, m, 1024), BF)], sums[c], after=after, name="halve"
        )
        sums[c] = keep, to_second(send)

    def spread(c, *after):
        m = len(CHUNKS[c]) * QR
        [own] = queue(terms, [((3, m, 1024), BF)], sums[c], after=after, name="terms")
        a1, a2 = to_second(own), to_first(own)
        parts[c] = [own, a1, a2, to_first(a1)]

    def back(c, *after):
        chunk = CHUNKS[c]
        n = len(chunk)
        rows = queue(
            functools.partial(back_rows, n),
            [((MR, DC), BF)] * n,
            (info, *parts[c], gate_proj, up_proj, others),
            [((n * MR, 1024), BF)] * 2,
            after=after,
            name="back_rows",
        )
        for d, r in zip(chunk, rows):
            returned[d] = r if d == 0 else along_x(r, NX - d)

    multiply(0)
    reduce(0)
    multiply(1)
    multiply(2, sums[0][1])
    reduce(1)
    reduce(2)
    spread(1)
    spread(2)
    spread(0, *parts[1][:3])
    back(1, *parts[2][:3])
    back(2, *parts[0][:3])
    back(0, returned[1], returned[3])

    home, mine, theirs = queue(
        combine,
        [((TB, DC), F32), ((448, DC), F32), ((448, DC), BF)],
        (info, slots, *returned),
        [((4 * MR, DC), BF), ((4 * MR, 1024), BF), ((TB, DC), F32)],
        name="combine",
    )
    homeward = queue(
        join,
        [block] * 3 + [((TB // 2, DC), BF)],
        (mine, swap(theirs)),
        name="join",
    )
    homed = [along_z(v, -far) for v, far in zip(homeward, (1, 2, 3, 4))]

    grad_gate, grad_up, grad_down, send = queue(
        weight_grads,
        [((2, DC, FH), BF), ((2, DC, FH), BF), ((2, FH, DC), BF), weights],
        (info, *messages, *[a for part in parts for a in part]),
        [((4 * MR, 2 * DC), BF), ((3, 4 * MR, 1024), BF)],
        name="weight_grads",
    )
    total, send = queue(
        bring_home, [((TB, DC), F32)], (info, home, *homed), hand=(send,), name="bring_home"
    )
    [grad_tokens] = queue(finish, [block], (total, swap(total)), name="finish")
    shape = jax.ShapeDtypeStruct
    grad_gate, grad_up, grad_down = pl.pallas_call(
        place_grads,
        out_shape=[shape(v.shape, BF) for v in (grad_gate, grad_up, grad_down)],
        in_specs=[SMEM, VMEM] + [ANY] * 4,
        out_specs=[ANY] * 3,
        scratch_shapes=[pltpu.SemaphoreType.DMA((4,))],
        input_output_aliases={2: 0, 3: 1, 4: 2},
        compiler_params=pltpu.CompilerParams(vmem_limit_bytes=48 * 2**20),
        cost_estimate=pl.CostEstimate(flops=0, bytes_accessed=6_000_000, transcendentals=0),
        name="place_grads",
    )(info, swap(send), grad_gate, grad_up, grad_down, grad_tokens)
    return grad_tokens, grad_gate, grad_up, grad_down


def solution(mesh):
    parts = Mesh(mesh.devices.reshape(NY, 2, NX, NZ), ("dp", "seq", "ex", "ez"))
    expert = ("ex", "ez")
    in_specs = (
        P(expert, "dp"),
        P(expert, "dp"),
        P(expert, None),
        P(expert, None),
        P(expert, "dp", "seq"),
        P(expert, "dp", "seq"),
        P(expert, "seq", "dp"),
    )
    out_specs = (
        P(expert, "dp"),
        P(expert, "dp", "seq"),
        P(expert, "dp", "seq"),
        P(expert, "seq", "dp"),
    )
    return jax.shard_map(
        on_device, mesh=parts, in_specs=in_specs, out_specs=out_specs, check_vma=False
    )
```

```python
import functools
import jax
import jax.numpy as jnp
from jax import lax
from jax.experimental import pallas as pl
from jax.experimental.pallas import tpu as pltpu
from jax.sharding import Mesh, PartitionSpec as P

BF = jnp.bfloat16
F32 = jnp.float32
NX, NZ, NY = 4, 8, 4
TB = 128
CAP = 24
QR = 48
MR = 192
DC = 896
FH = 512
META = 128
CHUNKS = ((0,), (1, 3), (2,))
VMEM = pl.BlockSpec(memory_space=pltpu.VMEM)
SMEM = pl.BlockSpec(memory_space=pltpu.SMEM)
NN = (((1,), (0,)), ((), ()))
NT = (((1,), (1,)), ((), ()))
TN = (((0,), (0,)), ((), ()))


def dot(a, b, dims=NN):
    return lax.dot_general(a, b, dims, preferred_element_type=F32)


ANY = pl.BlockSpec(memory_space=pl.ANY)


class Queue:
    def __init__(self):
        self.last = None

    def __call__(
        self, body, outs, ins, scratch=(), name=None, after=(), hand=(), hbm=False, limit=48, free=False
    ):
        waits = list(after) + ([] if free or self.last is None else [self.last])
        n, k, h, m = len(ins), len(waits), len(hand), len(outs)

        def run(*refs):
            body(*refs[:n], *refs[n + k + h : n + k + h + m], *refs[n + k + 2 * h + m :])

        done = pl.pallas_call(
            run,
            out_shape=[jax.ShapeDtypeStruct(s, t) for s, t in outs]
            + [jax.ShapeDtypeStruct(v.shape, v.dtype) for v in hand],
            in_specs=[SMEM if v.shape == (9,) else ANY if hbm else VMEM for v in ins]
            + [ANY] * (k + h),
            out_specs=[VMEM] * m + [ANY] * h,
            scratch_shapes=[pltpu.VMEM(*v) if isinstance(v, tuple) else v for v in scratch],
            input_output_aliases={n + k + i: m + i for i in range(h)},
            compiler_params=pltpu.CompilerParams(vmem_limit_bytes=limit * 2**20),
            cost_estimate=pl.CostEstimate(flops=1, bytes_accessed=1, transcendentals=0),
            name=name,
        )(*ins, *waits, *hand)
        if not free:
            self.last = done[0]
        return done


def first(y, s):
    return y ^ 1 if s == 0 else 3 - y


def second(y, s):
    return 3 - y if s == 0 else y ^ 1


def to_first(v):
    return lax.ppermute(
        v, ("dp", "seq"), [(y * 2 + s, first(y, s) * 2 + s) for y in range(NY) for s in range(2)]
    )


def to_second(v):
    return lax.ppermute(
        v, ("dp", "seq"), [(y * 2 + s, second(y, s) * 2 + s) for y in range(NY) for s in range(2)]
    )


def along_z(v, far):
    pairs = [(z, (z + far) % NZ) for z in range(NZ)]
    pairs += [(NZ + z, NZ + (z - far) % NZ) for z in range(NZ)]
    return lax.ppermute(v, ("seq", "ez"), pairs)


def opposite(v):
    pairs = [(z, (z + 2) % NZ) for z in range(0, NZ, 2)]
    pairs += [(NZ + z, NZ + (z - 2) % NZ) for z in range(1, NZ, 2)]
    return lax.ppermute(v, ("seq", "ez"), pairs)


def swap_opposite(v):
    pairs = [(z, NZ + z) if z % 2 == 0 else (NZ + z, z) for z in range(NZ)]
    return lax.ppermute(v, ("seq", "ez"), pairs)


def along_x(v, far):
    return lax.ppermute(v, "ex", [(x, (x + far) % NX) for x in range(NX)])


def swap(v):
    return lax.ppermute(v, "seq", [(0, 1), (1, 0)])


def copy_all(pairs, sems):
    copies = [pltpu.make_async_copy(a, b, sems.at[i]) for i, (a, b) in enumerate(pairs)]
    for copy in copies:
        copy.start()
    for copy in copies:
        copy.wait()


def half_of(gate, up, down, t, out):
    return (
        (gate.at[t], out.at[:DC]),
        (up.at[t], out.at[DC : 2 * DC]),
        (down.at[t, :, :FH], out.at[2 * DC : 2 * DC + FH]),
        (down.at[t, :, FH:], out.at[2 * DC + FH :, : DC - FH]),
    )


def pack(info, tokens, cot, ids, gates, gate, up, down, out, weights, numbers, scale, meta, sems):
    copies = [
        pltpu.make_async_copy(a, b, sems.at[i])
        for i, (a, b) in enumerate(
            (
                (ids, numbers),
                (gates, scale),
                (tokens, out.at[:, :DC]),
                (cot, out.at[:, DC : 2 * DC]),
                *half_of(gate, up, down, 1 - info[8], weights),
            )
        )
    ]
    for copy in copies:
        copy.start()
    meta[...] = jnp.zeros_like(meta)
    weights[2 * DC + FH :, DC - FH :] = jnp.zeros((FH, 2 * FH - DC), BF)
    copies[0].wait()
    copies[1].wait()
    high = scale[...].astype(BF).astype(F32)
    middle = (scale[...] - high).astype(BF).astype(F32)
    meta[0:8] = numbers[...].astype(F32)
    meta[8:16] = high
    meta[16:24] = middle
    meta[24:32] = (scale[...] - high) - middle
    out[:, 2 * DC :] = jnp.transpose(meta[...]).astype(BF)
    for copy in copies[2:]:
        copy.wait()


def pack_own(info, gate, up, down, out, sems):
    copy_all(half_of(gate, up, down, info[8], out), sems)
    out[2 * DC + FH :, DC - FH :] = jnp.zeros((FH, 2 * FH - DC), BF)


def place_grads(info, got, gate, up, down, token, gate_out, up_out, down_out, sems):
    t = 1 - info[8]
    copy_all(
        (
            (got.at[:DC], gate_out.at[t]),
            (got.at[DC : 2 * DC], up_out.at[t]),
            (got.at[2 * DC : 2 * DC + FH], down_out.at[t, :, :FH]),
            (got.at[2 * DC + FH :, : DC - FH], down_out.at[t, :, FH:]),
        ),
        sems,
    )


def bring_home(info, home, h1, h2, h3, h4, out):
    out[...] = home[...] + h1[...].astype(F32) + h2[...].astype(F32) + h3[...].astype(F32)
    at = pl.ds(pl.multiple_of(info[8] * (TB // 2), TB // 2), TB // 2)
    out[at] = out[at] + h4[...].astype(F32)


def finish(mine, other, out, token):
    token[...] = jnp.zeros_like(token)
    out[...] = (mine[...] + other[...]).astype(BF)


def put_down(out, down):
    out[2 * DC : 2 * DC + FH] = down[:, :FH]
    out[2 * DC + FH :, : DC - FH] = down[:, FH:]
    out[2 * DC + FH :, DC - FH :] = jnp.zeros((FH, 2 * FH - DC), BF)


def marks(slots, hot, q):
    masks = []
    for d in range(NX):
        for b in (2 * q, 2 * q + 1):
            at = d * NZ + b
            row = slots[at : at + 1, :]
            mask = lax.broadcasted_iota(jnp.int32, (QR, TB), 0).astype(F32) == row
            side = (b % 2) * TB
            hot[d * QR : (d + 1) * QR, side : side + TB] = mask.astype(F32).astype(BF)
            masks.append((at, mask))
    return masks


def pick(info, own, r1, r2, r3, r4, s4, s1, s2, s3, m0, m1, m2, m3, slots, rows, taken, gates, hot):
    for b, block in enumerate((own, r1, r2, r3, r4, s1, s2, s3)):
        at = slice(b * TB, (b + 1) * TB)
        if b == 4:
            rows[at] = r4[:, : 2 * DC] + s4[:, : 2 * DC]
            meta = r4[:, 2 * DC :] + s4[:, 2 * DC :]
        else:
            rows[at] = block[:, : 2 * DC]
            meta = block[:, 2 * DC :]
        turned = jnp.transpose(meta.astype(F32))
        ids = turned[0:8]
        gate = turned[8:16] + turned[16:24] + turned[24:32]
        for d in range(NX):
            named = ids == info[d].astype(F32)
            at = slice(d * NZ + b, d * NZ + b + 1)
            taken[at, :] = jnp.sum(named.astype(F32), axis=0, keepdims=True)
            gates[at, :] = jnp.sum(jnp.where(named, gate, 0.0), axis=0, keepdims=True)
    upper = lax.broadcasted_iota(jnp.int32, (TB, TB), 0) < lax.broadcasted_iota(
        jnp.int32, (TB, TB), 1
    )
    rank = dot(taken[...].astype(BF), upper.astype(F32).astype(BF))
    odd = lax.broadcasted_iota(jnp.int32, (NX * NZ, TB), 0) % 2
    slots[...] = jnp.where(taken[...] > 0.5, rank + (odd * CAP).astype(F32), -1.0)
    for q in range(4):
        found = [
            jnp.where(mask, gates[at : at + 1, :], 0.0) for at, mask in marks(slots, hot, q)
        ]
        tokens = slice(2 * q * TB, 2 * (q + 1) * TB)
        x = dot(hot[...], rows[tokens, :DC]).astype(BF)
        w = dot(hot[...], rows[tokens, DC:])
        place = pl.ds(pl.multiple_of(info[4 + q], QR), QR)
        for d, out in enumerate((m0, m1, m2, m3)):
            gate = jnp.sum(found[2 * d] + found[2 * d + 1], axis=1, keepdims=True)
            part = slice(d * QR, (d + 1) * QR)
            out[place, :DC] = x[part]
            out[place, DC:] = (gate * w[part]).astype(BF)


def combine(info, slots, b0, b1, b2, b3, own, mine, theirs, rows, hot, far):
    half = TB // 2
    for q in range(4):
        marks(slots, hot, q)
        place = pl.ds(pl.multiple_of(info[4 + q], QR), QR)
        for d, ref in enumerate((b0, b1, b2, b3)):
            rows[d * QR : (d + 1) * QR] = ref[place]
        for b in (2 * q, 2 * q + 1):
            side = (b % 2) * TB
            part = dot(hot[:, side : side + TB], rows[...], TN)
            if b == 0:
                own[...] = part
            elif b < 4:
                mine[(b - 1) * TB : b * TB] = part
            elif b == 4:
                far[...] = part
                mine[3 * TB :] = far[pl.ds(pl.multiple_of(info[8] * half, half), half)]
                theirs[3 * TB :] = far[
                    pl.ds(pl.multiple_of((1 - info[8]) * half, half), half)
                ].astype(BF)
            else:
                theirs[(b - 5) * TB : (b - 4) * TB] = part.astype(BF)


def join(mine, got, o1, o2, o3, o4):
    for i, out in enumerate((o1, o2, o3)):
        at = slice(i * TB, (i + 1) * TB)
        out[...] = (mine[at] + got[at].astype(F32)).astype(BF)
    o4[...] = (mine[384:448] + got[384:448].astype(F32)).astype(BF)


def by_quarter(dst, refs, start=0):
    n = len(refs)
    for q in range(4):
        for i, ref in enumerate(refs):
            dst[start + (q * n + i) * QR : start + (q * n + i + 1) * QR] = ref[
                q * QR : (q + 1) * QR
            ]


def products(n, *refs):
    messages, (own, other, keep, send, rows) = refs[:n], refs[n:]
    by_quarter(rows, messages)
    x, w = rows[:, :DC], rows[:, DC:]
    half = n * 2 * QR
    down = 2 * DC
    for at, part in ((0, own), (FH, other)):
        for k, v in (
            (0, dot(x, part[:DC])),
            (1, dot(x, part[DC:down])),
            (
                2,
                dot(w[:, :FH], part[down : down + FH], NT)
                + dot(w[:, FH:], part[down + FH :, : DC - FH], NT),
            ),
        ):
            keep[k, :, at : at + FH] = v[:half]
            send[k, :, at : at + FH] = v[half:].astype(BF)


def halve(keep, got, mine, send):
    m = keep.shape[-2] // 2
    mine[...] = keep[..., :m, :] + got[..., :m, :].astype(F32)
    send[...] = (keep[..., m:, :] + got[..., m:, :].astype(F32)).astype(BF)


def terms(keep, got, out):
    g = keep[0] + got[0].astype(F32)
    u = keep[1] + got[1].astype(F32)
    h = keep[2] + got[2].astype(F32)
    s = jax.nn.sigmoid(g)
    act = g * s
    out[0] = (act * u).astype(BF)
    out[1] = (h * u * s * (1.0 + g * (1.0 - s))).astype(BF)
    out[2] = (h * act).astype(BF)


def back_rows(n, a0, a1, a2, a3, own, other, *refs):
    outs, (dg, du) = refs[:n], refs[n:]
    m = n * QR
    for q, a in enumerate((a0, a1, a2, a3)):
        dg[q * m : (q + 1) * m] = a[1]
        du[q * m : (q + 1) * m] = a[2]
    total = dot(dg[:, :FH], own[:DC], NT) + dot(dg[:, FH:], other[:DC], NT)
    total = total + dot(du[:, :FH], own[DC : 2 * DC], NT) + dot(du[:, FH:], other[DC : 2 * DC], NT)
    total = total.astype(BF)
    for q in range(4):
        for i, out in enumerate(outs):
            out[q * QR : (q + 1) * QR] = total[(q * n + i) * QR : (q * n + i + 1) * QR]


def weight_grads(info, *refs):
    messages, parts = refs[:4], refs[4 : 4 + 4 * len(CHUNKS)]
    token, gate, up, down, send, rows, cols = refs[4 + 4 * len(CHUNKS) :]
    s = info[8]
    token[...] = jnp.zeros_like(token)
    start = 0
    for c, chunk in enumerate(CHUNKS):
        n = len(chunk)
        by_quarter(rows, [messages[d] for d in chunk], start)
        for q in range(4):
            at = start + q * n * QR
            cols[:, at : at + n * QR] = parts[4 * c + q][...]
        start += n * MR
    x, w = rows[:, :DC], rows[:, DC:]
    down[s] = dot(cols[0, :, :FH], w, TN).astype(BF)
    put_down(send, dot(cols[0, :, FH:], w, TN).astype(BF))
    gate[s] = dot(x, cols[1, :, :FH], TN).astype(BF)
    send[:DC] = dot(x, cols[1, :, FH:], TN).astype(BF)
    up[s] = dot(x, cols[2, :, :FH], TN).astype(BF)
    send[DC : 2 * DC] = dot(x, cols[2, :, FH:], TN).astype(BF)


def on_device(tokens, cotangent, expert_ids, gate_weights, gate_proj, up_proj, down_proj):
    y, s = lax.axis_index("dp"), lax.axis_index("seq")
    x, z = lax.axis_index("ex"), lax.axis_index("ez")
    p1 = jnp.where(s == 0, y ^ 1, 3 - y)
    p2 = jnp.where(s == 0, 3 - y, y ^ 1)
    experts = [2 * (((x + d) % NX) * NZ + z) + s for d in range(NX)]
    bases = [
        QR * jnp.where(q == y, 0, jnp.where(q == p2, 1, jnp.where(q == p1, 2, 3)))
        for q in range(4)
    ]
    info = jnp.stack([jnp.asarray(v, jnp.int32) for v in [*experts, *bases, s]])

    queue = Queue()
    block, token = ((TB, DC), BF), ((8, TB), F32)

    weights = ((2 * DC + 2 * FH, FH), BF)
    message = ((MR, 2 * DC), BF)
    width = 2 * DC + META

    packed, others = queue(
        pack,
        [((TB, width), BF), weights],
        (
            info,
            tokens,
            cotangent,
            expert_ids.T,
            gate_weights.T,
            gate_proj,
            up_proj,
            down_proj,
        ),
        [
            ((8, TB), jnp.int32),
            ((8, TB), F32),
            ((META, TB), F32),
            pltpu.SemaphoreType.DMA((8,)),
        ],
        name="pack",
        hbm=True,
        limit=60,
    )
    r1, r2 = along_z(packed, 1), along_z(packed, 2)
    own_weights, r1 = queue(
        pack_own,
        [weights],
        (info, gate_proj, up_proj, down_proj),
        [pltpu.SemaphoreType.DMA((4,))],
        name="pack_own",
        hand=(r1,),
        hbm=True,
        limit=60,
        free=True,
    )
    r3, r4 = along_z(r2, 1), opposite(r2)
    others = swap(others)
    *messages, slots = queue(
        pick,
        [message] * 4 + [((32, TB), F32)],
        (info, packed, r1, r2, r3, r4, swap_opposite(r4), swap(r1), swap(r2), swap(r3)),
        [((1024, 2 * DC), BF), ((32, TB), F32), ((32, TB), F32), ((MR, 2 * TB), BF)],
        name="pick",
    )
    messages = [m if d == 0 else along_x(m, d) for d, m in enumerate(messages)]

    count = len(CHUNKS)
    sums, parts, returned = [None] * count, [None] * count, [None] * NX

    def multiply(c, *after):
        chunk = CHUNKS[c]
        n = len(chunk)
        keep, send = queue(
            functools.partial(products, n),
            [((3, n * 2 * QR, 1024), F32), ((3, n * 2 * QR, 1024), BF)],
            (*[messages[d] for d in chunk], own_weights, others),
            [((n * MR, 2 * DC), BF)],
            after=after,
            name="products",
        )
        sums[c] = keep, to_first(send)

    def reduce(c, *after):
        m = len(CHUNKS[c]) * QR
        keep, send = queue(
            halve, [((3, m, 1024), F32), ((3, m, 1024), BF)], sums[c], after=after, name="halve"
        )
        sums[c] = keep, to_second(send)

    def spread(c, *after):
        m = len(CHUNKS[c]) * QR
        [own] = queue(terms, [((3, m, 1024), BF)], sums[c], after=after, name="terms")
        a1, a2 = to_second(own), to_first(own)
        parts[c] = [own, a1, a2, to_first(a1)]

    def back(c, *after):
        chunk = CHUNKS[c]
        n = len(chunk)
        rows = queue(
            functools.partial(back_rows, n),
            [((MR, DC), BF)] * n,
            (*parts[c], own_weights, others),
            [((n * MR, 1024), BF)] * 2,
            after=after,
            name="back_rows",
        )
        for d, r in zip(chunk, rows):
            returned[d] = r if d == 0 else along_x(r, NX - d)

    multiply(0)
    reduce(0)
    multiply(1)
    multiply(2, sums[0][1])
    reduce(1)
    reduce(2)
    spread(1)
    spread(2)
    spread(0, *parts[1][:3])
    back(1, *parts[2][:3])
    back(2, *parts[0][:3])
    back(0, returned[1], returned[3])

    home, mine, theirs = queue(
        combine,
        [((TB, DC), F32), ((448, DC), F32), ((448, DC), BF)],
        (info, slots, *returned),
        [((MR, DC), BF), ((MR, 2 * TB), BF), ((TB, DC), F32)],
        name="combine",
    )
    homeward = queue(
        join,
        [block] * 3 + [((TB // 2, DC), BF)],
        (mine, swap(theirs)),
        name="join",
    )
    homed = [along_z(v, -far) for v, far in zip(homeward, (1, 2, 3, 4))]

    _, grad_gate, grad_up, grad_down, send = queue(
        weight_grads,
        [token, ((2, DC, FH), BF), ((2, DC, FH), BF), ((2, FH, DC), BF), weights],
        (info, *messages, *[a for part in parts for a in part]),
        [((4 * MR, 2 * DC), BF), ((3, 4 * MR, 1024), BF)],
        name="weight_grads",
    )
    total, send = queue(
        bring_home, [((TB, DC), F32)], (info, home, *homed), hand=(send,), name="bring_home"
    )
    grad_tokens, last = queue(finish, [block, token], (total, swap(total)), name="finish")
    shape = jax.ShapeDtypeStruct
    grad_gate, grad_up, grad_down = pl.pallas_call(
        place_grads,
        out_shape=[shape(v.shape, BF) for v in (grad_gate, grad_up, grad_down)],
        in_specs=[SMEM, VMEM] + [ANY] * 4,
        out_specs=[ANY] * 3,
        scratch_shapes=[pltpu.SemaphoreType.DMA((4,))],
        input_output_aliases={2: 0, 3: 1, 4: 2},
        compiler_params=pltpu.CompilerParams(vmem_limit_bytes=48 * 2**20),
        cost_estimate=pl.CostEstimate(flops=0, bytes_accessed=6_000_000, transcendentals=0),
        name="place_grads",
    )(info, swap(send), grad_gate, grad_up, grad_down, last)
    return grad_tokens, grad_gate, grad_up, grad_down


def solution(mesh):
    parts = Mesh(mesh.devices.reshape(NY, 2, NX, NZ), ("dp", "seq", "ex", "ez"))
    expert = ("ex", "ez")
    in_specs = (
        P(expert, "dp"),
        P(expert, "dp"),
        P(expert, None),
        P(expert, None),
        P(expert, "dp", "seq"),
        P(expert, "dp", "seq"),
        P(expert, "seq", "dp"),
    )
    out_specs = (
        P(expert, "dp"),
        P(expert, "dp", "seq"),
        P(expert, "dp", "seq"),
        P(expert, "seq", "dp"),
    )
    return jax.shard_map(
        on_device, mesh=parts, in_specs=in_specs, out_specs=out_specs, check_vma=False
    )
```

```python
import functools
import jax
import jax.numpy as jnp
from jax import lax
from jax.experimental import pallas as pl
from jax.experimental.pallas import tpu as pltpu
from jax.sharding import Mesh, PartitionSpec as P

BF = jnp.bfloat16
F32 = jnp.float32
NX, NZ, NY = 4, 8, 4
TB = 128
CAP = 24
QR = 48
MR = 192
DC = 896
FH = 512
META = 128
CHUNKS = ((0,), (1, 3), (2,))
VMEM = pl.BlockSpec(memory_space=pltpu.VMEM)
SMEM = pl.BlockSpec(memory_space=pltpu.SMEM)
NN = (((1,), (0,)), ((), ()))
NT = (((1,), (1,)), ((), ()))
TN = (((0,), (0,)), ((), ()))


def dot(a, b, dims=NN):
    return lax.dot_general(a, b, dims, preferred_element_type=F32)


ANY = pl.BlockSpec(memory_space=pl.ANY)


class Queue:
    def __init__(self):
        self.last = None

    def __call__(
        self, body, outs, ins, scratch=(), name=None, after=(), hand=(), hbm=False, limit=24, free=False
    ):
        waits = list(after) + ([] if free or self.last is None else [self.last])
        n, k, h, m = len(ins), len(waits), len(hand), len(outs)

        def run(*refs):
            body(*refs[:n], *refs[n + k + h : n + k + h + m], *refs[n + k + 2 * h + m :])

        done = pl.pallas_call(
            run,
            out_shape=[jax.ShapeDtypeStruct(s, t) for s, t in outs]
            + [jax.ShapeDtypeStruct(v.shape, v.dtype) for v in hand],
            in_specs=[SMEM if v.shape == (9,) else ANY if hbm else VMEM for v in ins]
            + [ANY] * (k + h),
            out_specs=[VMEM] * m + [ANY] * h,
            scratch_shapes=[pltpu.VMEM(*v) if isinstance(v, tuple) else v for v in scratch],
            input_output_aliases={n + k + i: m + i for i in range(h)},
            compiler_params=pltpu.CompilerParams(vmem_limit_bytes=limit * 2**20),
            cost_estimate=pl.CostEstimate(flops=1, bytes_accessed=1, transcendentals=0),
            name=name,
        )(*ins, *waits, *hand)
        if not free:
            self.last = done[0]
        return done


def first(y, s):
    return y ^ 1 if s == 0 else 3 - y


def second(y, s):
    return 3 - y if s == 0 else y ^ 1


def to_first(v):
    return lax.ppermute(
        v, ("dp", "seq"), [(y * 2 + s, first(y, s) * 2 + s) for y in range(NY) for s in range(2)]
    )


def to_second(v):
    return lax.ppermute(
        v, ("dp", "seq"), [(y * 2 + s, second(y, s) * 2 + s) for y in range(NY) for s in range(2)]
    )


def along_z(v, far):
    pairs = [(z, (z + far) % NZ) for z in range(NZ)]
    pairs += [(NZ + z, NZ + (z - far) % NZ) for z in range(NZ)]
    return lax.ppermute(v, ("seq", "ez"), pairs)


def opposite(v):
    pairs = [(z, (z + 2) % NZ) for z in range(0, NZ, 2)]
    pairs += [(NZ + z, NZ + (z - 2) % NZ) for z in range(1, NZ, 2)]
    return lax.ppermute(v, ("seq", "ez"), pairs)


def swap_opposite(v):
    pairs = [(z, NZ + z) if z % 2 == 0 else (NZ + z, z) for z in range(NZ)]
    return lax.ppermute(v, ("seq", "ez"), pairs)


def along_x(v, far):
    return lax.ppermute(v, "ex", [(x, (x + far) % NX) for x in range(NX)])


def swap(v):
    return lax.ppermute(v, "seq", [(0, 1), (1, 0)])


def copy_all(pairs, sems):
    copies = [pltpu.make_async_copy(a, b, sems.at[i]) for i, (a, b) in enumerate(pairs)]
    for copy in copies:
        copy.start()
    for copy in copies:
        copy.wait()


def half_of(gate, up, down, t, out):
    return (
        (gate.at[t], out.at[:DC]),
        (up.at[t], out.at[DC : 2 * DC]),
        (down.at[t, :, :FH], out.at[2 * DC : 2 * DC + FH]),
        (down.at[t, :, FH:], out.at[2 * DC + FH :, : DC - FH]),
    )


def pack(info, tokens, cot, ids, gates, gate, up, down, out, weights, numbers, scale, meta, sems):
    copies = [
        pltpu.make_async_copy(a, b, sems.at[i])
        for i, (a, b) in enumerate(
            (
                (ids, numbers),
                (gates, scale),
                (tokens, out.at[:, :DC]),
                (cot, out.at[:, DC : 2 * DC]),
                *half_of(gate, up, down, 1 - info[8], weights),
            )
        )
    ]
    for copy in copies:
        copy.start()
    meta[...] = jnp.zeros_like(meta)
    weights[2 * DC + FH :, DC - FH :] = jnp.zeros((FH, 2 * FH - DC), BF)
    copies[0].wait()
    copies[1].wait()
    high = scale[...].astype(BF).astype(F32)
    middle = (scale[...] - high).astype(BF).astype(F32)
    meta[0:8] = numbers[...].astype(F32)
    meta[8:16] = high
    meta[16:24] = middle
    meta[24:32] = (scale[...] - high) - middle
    out[:, 2 * DC :] = jnp.transpose(meta[...]).astype(BF)
    for copy in copies[2:]:
        copy.wait()


def pack_own(info, gate, up, down, out, sems):
    copy_all(half_of(gate, up, down, info[8], out), sems)
    out[2 * DC + FH :, DC - FH :] = jnp.zeros((FH, 2 * FH - DC), BF)


def place_grads(info, got, gate, up, down, token, gate_out, up_out, down_out, sems):
    t = 1 - info[8]
    copy_all(
        (
            (got.at[:DC], gate_out.at[t]),
            (got.at[DC : 2 * DC], up_out.at[t]),
            (got.at[2 * DC : 2 * DC + FH], down_out.at[t, :, :FH]),
            (got.at[2 * DC + FH :, : DC - FH], down_out.at[t, :, FH:]),
        ),
        sems,
    )


def bring_home(info, home, h1, h2, h3, h4, out):
    out[...] = home[...] + h1[...].astype(F32) + h2[...].astype(F32) + h3[...].astype(F32)
    at = pl.ds(pl.multiple_of(info[8] * (TB // 2), TB // 2), TB // 2)
    out[at] = out[at] + h4[...].astype(F32)


def finish(mine, other, out, token):
    token[...] = jnp.zeros_like(token)
    out[...] = (mine[...] + other[...]).astype(BF)


def put_down(out, down):
    out[2 * DC : 2 * DC + FH] = down[:, :FH]
    out[2 * DC + FH :, : DC - FH] = down[:, FH:]
    out[2 * DC + FH :, DC - FH :] = jnp.zeros((FH, 2 * FH - DC), BF)


def marks(slots, hot, q):
    masks = []
    for d in range(NX):
        for b in (2 * q, 2 * q + 1):
            at = d * NZ + b
            row = slots[at : at + 1, :]
            mask = lax.broadcasted_iota(jnp.int32, (QR, TB), 0).astype(F32) == row
            side = (b % 2) * TB
            hot[d * QR : (d + 1) * QR, side : side + TB] = mask.astype(F32).astype(BF)
            masks.append((at, mask))
    return masks


def pick(info, own, r1, r2, r3, r4, s4, s1, s2, s3, m0, m1, m2, m3, slots, rows, taken, gates, hot):
    for b, block in enumerate((own, r1, r2, r3, r4, s1, s2, s3)):
        at = slice(b * TB, (b + 1) * TB)
        if b == 4:
            rows[at] = r4[:, : 2 * DC] + s4[:, : 2 * DC]
            meta = r4[:, 2 * DC :] + s4[:, 2 * DC :]
        else:
            rows[at] = block[:, : 2 * DC]
            meta = block[:, 2 * DC :]
        turned = jnp.transpose(meta.astype(F32))
        ids = turned[0:8]
        gate = turned[8:16] + turned[16:24] + turned[24:32]
        for d in range(NX):
            named = ids == info[d].astype(F32)
            at = slice(d * NZ + b, d * NZ + b + 1)
            taken[at, :] = jnp.sum(named.astype(F32), axis=0, keepdims=True)
            gates[at, :] = jnp.sum(jnp.where(named, gate, 0.0), axis=0, keepdims=True)
    upper = lax.broadcasted_iota(jnp.int32, (TB, TB), 0) < lax.broadcasted_iota(
        jnp.int32, (TB, TB), 1
    )
    rank = dot(taken[...].astype(BF), upper.astype(F32).astype(BF))
    odd = lax.broadcasted_iota(jnp.int32, (NX * NZ, TB), 0) % 2
    slots[...] = jnp.where(taken[...] > 0.5, rank + (odd * CAP).astype(F32), -1.0)
    for q in range(4):
        found = [
            jnp.where(mask, gates[at : at + 1, :], 0.0) for at, mask in marks(slots, hot, q)
        ]
        tokens = slice(2 * q * TB, 2 * (q + 1) * TB)
        x = dot(hot[...], rows[tokens, :DC]).astype(BF)
        w = dot(hot[...], rows[tokens, DC:])
        place = pl.ds(pl.multiple_of(info[4 + q], QR), QR)
        for d, out in enumerate((m0, m1, m2, m3)):
            gate = jnp.sum(found[2 * d] + found[2 * d + 1], axis=1, keepdims=True)
            part = slice(d * QR, (d + 1) * QR)
            out[place, :DC] = x[part]
            out[place, DC:] = (gate * w[part]).astype(BF)


def combine(info, slots, b0, b1, b2, b3, own, mine, theirs, rows, hot, far):
    half = TB // 2
    for q in range(4):
        marks(slots, hot, q)
        place = pl.ds(pl.multiple_of(info[4 + q], QR), QR)
        for d, ref in enumerate((b0, b1, b2, b3)):
            rows[d * QR : (d + 1) * QR] = ref[place]
        for b in (2 * q, 2 * q + 1):
            side = (b % 2) * TB
            part = dot(hot[:, side : side + TB], rows[...], TN)
            if b == 0:
                own[...] = part
            elif b < 4:
                mine[(b - 1) * TB : b * TB] = part
            elif b == 4:
                far[...] = part
                mine[3 * TB :] = far[pl.ds(pl.multiple_of(info[8] * half, half), half)]
                theirs[3 * TB :] = far[
                    pl.ds(pl.multiple_of((1 - info[8]) * half, half), half)
                ].astype(BF)
            else:
                theirs[(b - 5) * TB : (b - 4) * TB] = part.astype(BF)


def join(mine, got, o1, o2, o3, o4):
    for i, out in enumerate((o1, o2, o3)):
        at = slice(i * TB, (i + 1) * TB)
        out[...] = (mine[at] + got[at].astype(F32)).astype(BF)
    o4[...] = (mine[384:448] + got[384:448].astype(F32)).astype(BF)


def by_quarter(dst, refs, start=0):
    n = len(refs)
    for q in range(4):
        for i, ref in enumerate(refs):
            dst[start + (q * n + i) * QR : start + (q * n + i + 1) * QR] = ref[
                q * QR : (q + 1) * QR
            ]


def products(n, *refs):
    messages, (own, other, keep, send, rows) = refs[:n], refs[n:]
    by_quarter(rows, messages)
    x, w = rows[:, :DC], rows[:, DC:]
    half = n * 2 * QR
    down = 2 * DC
    for at, part in ((0, own), (FH, other)):
        for k, v in (
            (0, dot(x, part[:DC])),
            (1, dot(x, part[DC:down])),
            (
                2,
                dot(w[:, :FH], part[down : down + FH], NT)
                + dot(w[:, FH:], part[down + FH :, : DC - FH], NT),
            ),
        ):
            keep[k, :, at : at + FH] = v[:half]
            send[k, :, at : at + FH] = v[half:].astype(BF)


def halve(keep, got, mine, send):
    m = keep.shape[-2] // 2
    mine[...] = keep[..., :m, :] + got[..., :m, :].astype(F32)
    send[...] = (keep[..., m:, :] + got[..., m:, :].astype(F32)).astype(BF)


def terms(keep, got, out):
    g = keep[0] + got[0].astype(F32)
    u = keep[1] + got[1].astype(F32)
    h = keep[2] + got[2].astype(F32)
    s = jax.nn.sigmoid(g)
    act = g * s
    out[0] = (act * u).astype(BF)
    out[1] = (h * u * s * (1.0 + g * (1.0 - s))).astype(BF)
    out[2] = (h * act).astype(BF)


def back_rows(n, a0, a1, a2, a3, own, other, *refs):
    outs, (dg, du) = refs[:n], refs[n:]
    m = n * QR
    for q, a in enumerate((a0, a1, a2, a3)):
        dg[q * m : (q + 1) * m] = a[1]
        du[q * m : (q + 1) * m] = a[2]
    total = dot(dg[:, :FH], own[:DC], NT) + dot(dg[:, FH:], other[:DC], NT)
    total = total + dot(du[:, :FH], own[DC : 2 * DC], NT) + dot(du[:, FH:], other[DC : 2 * DC], NT)
    total = total.astype(BF)
    for q in range(4):
        for i, out in enumerate(outs):
            out[q * QR : (q + 1) * QR] = total[(q * n + i) * QR : (q * n + i + 1) * QR]


def weight_grads(info, *refs):
    messages, parts = refs[:4], refs[4 : 4 + 4 * len(CHUNKS)]
    token, gate, up, down, send, rows, cols = refs[4 + 4 * len(CHUNKS) :]
    s = info[8]
    token[...] = jnp.zeros_like(token)
    start = 0
    for c, chunk in enumerate(CHUNKS):
        n = len(chunk)
        by_quarter(rows, [messages[d] for d in chunk], start)
        for q in range(4):
            at = start + q * n * QR
            cols[:, at : at + n * QR] = parts[4 * c + q][...]
        start += n * MR
    x, w = rows[:, :DC], rows[:, DC:]
    down[s] = dot(cols[0, :, :FH], w, TN).astype(BF)
    put_down(send, dot(cols[0, :, FH:], w, TN).astype(BF))
    gate[s] = dot(x, cols[1, :, :FH], TN).astype(BF)
    send[:DC] = dot(x, cols[1, :, FH:], TN).astype(BF)
    up[s] = dot(x, cols[2, :, :FH], TN).astype(BF)
    send[DC : 2 * DC] = dot(x, cols[2, :, FH:], TN).astype(BF)


def on_device(tokens, cotangent, expert_ids, gate_weights, gate_proj, up_proj, down_proj):
    y, s = lax.axis_index("dp"), lax.axis_index("seq")
    x, z = lax.axis_index("ex"), lax.axis_index("ez")
    p1 = jnp.where(s == 0, y ^ 1, 3 - y)
    p2 = jnp.where(s == 0, 3 - y, y ^ 1)
    experts = [2 * (((x + d) % NX) * NZ + z) + s for d in range(NX)]
    bases = [
        QR * jnp.where(q == y, 0, jnp.where(q == p2, 1, jnp.where(q == p1, 2, 3)))
        for q in range(4)
    ]
    info = jnp.stack([jnp.asarray(v, jnp.int32) for v in [*experts, *bases, s]])

    queue = Queue()
    block, token = ((TB, DC), BF), ((8, TB), F32)

    weights = ((2 * DC + 2 * FH, FH), BF)
    message = ((MR, 2 * DC), BF)
    width = 2 * DC + META

    packed, others = queue(
        pack,
        [((TB, width), BF), weights],
        (
            info,
            tokens,
            cotangent,
            expert_ids.T,
            gate_weights.T,
            gate_proj,
            up_proj,
            down_proj,
        ),
        [
            ((8, TB), jnp.int32),
            ((8, TB), F32),
            ((META, TB), F32),
            pltpu.SemaphoreType.DMA((8,)),
        ],
        name="pack",
        hbm=True,
        limit=60,
    )
    r1, r2 = along_z(packed, 1), along_z(packed, 2)
    own_weights, r1 = queue(
        pack_own,
        [weights],
        (info, gate_proj, up_proj, down_proj),
        [pltpu.SemaphoreType.DMA((4,))],
        name="pack_own",
        hand=(r1,),
        hbm=True,
        limit=60,
        free=True,
    )
    r3, r4 = along_z(r2, 1), opposite(r2)
    others = swap(others)
    *messages, slots = queue(
        pick,
        [message] * 4 + [((32, TB), F32)],
        (info, packed, r1, r2, r3, r4, swap_opposite(r4), swap(r1), swap(r2), swap(r3)),
        [((1024, 2 * DC), BF), ((32, TB), F32), ((32, TB), F32), ((MR, 2 * TB), BF)],
        name="pick",
    )
    messages = [m if d == 0 else along_x(m, d) for d, m in enumerate(messages)]

    count = len(CHUNKS)
    sums, parts, returned = [None] * count, [None] * count, [None] * NX

    def multiply(c, *after):
        chunk = CHUNKS[c]
        n = len(chunk)
        keep, send = queue(
            functools.partial(products, n),
            [((3, n * 2 * QR, 1024), F32), ((3, n * 2 * QR, 1024), BF)],
            (*[messages[d] for d in chunk], own_weights, others),
            [((n * MR, 2 * DC), BF)],
            after=after,
            name="products",
        )
        sums[c] = keep, to_first(send)

    def reduce(c, *after):
        m = len(CHUNKS[c]) * QR
        keep, send = queue(
            halve, [((3, m, 1024), F32), ((3, m, 1024), BF)], sums[c], after=after, name="halve"
        )
        sums[c] = keep, to_second(send)

    def spread(c, *after):
        m = len(CHUNKS[c]) * QR
        [own] = queue(terms, [((3, m, 1024), BF)], sums[c], after=after, name="terms")
        a1, a2 = to_second(own), to_first(own)
        parts[c] = [own, a1, a2, to_first(a1)]

    def back(c, *after):
        chunk = CHUNKS[c]
        n = len(chunk)
        rows = queue(
            functools.partial(back_rows, n),
            [((MR, DC), BF)] * n,
            (*parts[c], own_weights, others),
            [((n * MR, 1024), BF)] * 2,
            after=after,
            name="back_rows",
        )
        for d, r in zip(chunk, rows):
            returned[d] = r if d == 0 else along_x(r, NX - d)

    multiply(0)
    reduce(0)
    multiply(1)
    multiply(2, sums[0][1])
    reduce(1)
    reduce(2)
    spread(1)
    spread(0, *parts[1][1:3])
    spread(2)
    back(1, *parts[2][1:3])
    back(2, *parts[0][1:3])
    back(0, returned[1], returned[3])

    home, mine, theirs = queue(
        combine,
        [((TB, DC), F32), ((448, DC), F32), ((448, DC), BF)],
        (info, slots, *returned),
        [((MR, DC), BF), ((MR, 2 * TB), BF), ((TB, DC), F32)],
        name="combine",
    )
    homeward = queue(
        join,
        [block] * 3 + [((TB // 2, DC), BF)],
        (mine, swap(theirs)),
        name="join",
    )
    homed = [along_z(v, -far) for v, far in zip(homeward, (1, 2, 3, 4))]

    _, grad_gate, grad_up, grad_down, send = queue(
        weight_grads,
        [token, ((2, DC, FH), BF), ((2, DC, FH), BF), ((2, FH, DC), BF), weights],
        (info, *messages, *[a for part in parts for a in part]),
        [((4 * MR, 2 * DC), BF), ((3, 4 * MR, 1024), BF)],
        name="weight_grads",
        limit=48,
    )
    total, send = queue(
        bring_home, [((TB, DC), F32)], (info, home, *homed), hand=(send,), name="bring_home"
    )
    grad_tokens, last = queue(finish, [block, token], (total, swap(total)), name="finish")
    shape = jax.ShapeDtypeStruct
    grad_gate, grad_up, grad_down = pl.pallas_call(
        place_grads,
        out_shape=[shape(v.shape, BF) for v in (grad_gate, grad_up, grad_down)],
        in_specs=[SMEM, VMEM] + [ANY] * 4,
        out_specs=[ANY] * 3,
        scratch_shapes=[pltpu.SemaphoreType.DMA((4,))],
        input_output_aliases={2: 0, 3: 1, 4: 2},
        compiler_params=pltpu.CompilerParams(vmem_limit_bytes=48 * 2**20),
        cost_estimate=pl.CostEstimate(flops=0, bytes_accessed=6_000_000, transcendentals=0),
        name="place_grads",
    )(info, swap(send), grad_gate, grad_up, grad_down, last)
    return grad_tokens, grad_gate, grad_up, grad_down


def solution(mesh):
    parts = Mesh(mesh.devices.reshape(NY, 2, NX, NZ), ("dp", "seq", "ex", "ez"))
    expert = ("ex", "ez")
    in_specs = (
        P(expert, "dp"),
        P(expert, "dp"),
        P(expert, None),
        P(expert, None),
        P(expert, "dp", "seq"),
        P(expert, "dp", "seq"),
        P(expert, "seq", "dp"),
    )
    out_specs = (
        P(expert, "dp"),
        P(expert, "dp", "seq"),
        P(expert, "dp", "seq"),
        P(expert, "seq", "dp"),
    )
    return jax.shard_map(
        on_device, mesh=parts, in_specs=in_specs, out_specs=out_specs, check_vma=False
    )
```
